32 devices in a mesh: chan: 4 (over y, core), rng: 8 (over z, x).
Axes of the slice: x: 2, y: 2, z: 4, core: 2. Of those that a mesh axis runs over, the one named last changes fastest.
Arguments:
- echoes: float32 [2, 512, 64, 1024], P(None, 'chan', None, 'rng'), may hold values from -6 to 6
- filter_taps: float32 [2, 512], replicated, may hold values from -0.1875 to 0.1875
Outputs:
- covariance: float32 [2, 64, 512, 512], P(None, 'rng', 'chan')
The draws below stay inside these ranges and needn't reach their ends.
All inputs are finite; a program needn't handle non-finite values.
Results may differ from the reference program's by a relative error of at most 0.0003.
Values sent between devices are 32-bit elements; how exact they have to be, the bound alone decides.
A program may use at most 128 MiB of HBM per device.

```python
import math
import jax
import jax.numpy as jnp
from jax import lax

C = 512
P_SIZE = 64
TAPS = 512
GATES = 1024


def steps_of(key, dims, split, smallest, high):
    def one(position, blocks):
        draws = jax.random.uniform(jax.random.fold_in(jax.random.fold_in(key, 6), position), (blocks,), jnp.float32, smallest / len(split), high / len(split))
        return jnp.repeat(jnp.exp(draws), dims[position] // blocks).reshape((-1,) + (1,) * (len(dims) - position - 1))

    gain = one(*split[0])
    for cut in split[1:]:
        gain = gain * one(*cut)
    return gain


def gaussian(rng, extent, deviation, limit, split=(), kind=jnp.bfloat16):
    array = deviation * jax.random.normal(rng, extent, jnp.float32)
    if split:
        array = array * steps_of(rng, extent, split, -0.22, 0.18)
    return jnp.clip(array, -limit, limit).astype(kind)


def setup_inputs(seed: int = 0) -> dict:
    key_of = jax.random.split(jax.random.key(seed), 3)
    echoes = gaussian(key_of[0], (2, C, P_SIZE, GATES), 1.0, 6.0, ((1, 4), (3, 8)), jnp.float32)
    filter_taps = gaussian(key_of[1], (2, TAPS), (2 * TAPS) ** -0.5, 0.1875, (), jnp.float32)
    return dict(echoes=echoes, filter_taps=filter_taps)


def reference(echoes, filter_taps):
    pulse_count = echoes.shape[2]
    gate_count = echoes.shape[3]
    tap_count = filter_taps.shape[1]
    fft_len = gate_count + tap_count
    taps_cplx = filter_taps[0] + 1j * filter_taps[1]
    taps_spec = fft_len * jnp.fft.ifft(taps_cplx, n=fft_len)
    pulse_idx = jnp.arange(pulse_count, dtype=jnp.int32)
    norm_factor = 1.0 / math.sqrt(pulse_count)
    highest = lax.Precision.HIGHEST

    def one_bin(bin_index):
        phases = (bin_index * pulse_idx % pulse_count).astype(jnp.float32) * (2.0 * math.pi / pulse_count)
        cos_table = jnp.cos(phases)
        sin_table = jnp.sin(phases)
        spec_re = (jnp.einsum('cpg,p->cg', echoes[0], cos_table, precision=highest) + jnp.einsum('cpg,p->cg', echoes[1], sin_table, precision=highest)) * norm_factor
        spec_im = (jnp.einsum('cpg,p->cg', echoes[1], cos_table, precision=highest) - jnp.einsum('cpg,p->cg', echoes[0], sin_table, precision=highest)) * norm_factor
        filtered = jnp.fft.ifft(jnp.fft.fft(spec_re + 1j * spec_im, n=fft_len, axis=-1) * taps_spec, axis=-1)[:, :gate_count]
        out_re = jnp.real(filtered).astype(jnp.float32)
        out_im = jnp.imag(filtered).astype(jnp.float32)
        real_part = (jnp.dot(out_re, out_re.T, precision=highest, preferred_element_type=jnp.float32) + jnp.dot(out_im, out_im.T, precision=highest, preferred_element_type=jnp.float32)) / gate_count
        imag_part = (jnp.dot(out_im, out_re.T, precision=highest, preferred_element_type=jnp.float32) - jnp.dot(out_re, out_im.T, precision=highest, preferred_element_type=jnp.float32)) / gate_count
        return jnp.stack([real_part, imag_part])
    stacked = lax.map(one_bin, jnp.arange(pulse_count, dtype=jnp.int32))
    return jnp.transpose(stacked, (1, 0, 2, 3))
```

```python
import math

import jax
import jax.numpy as jnp
from jax import lax
from jax.sharding import PartitionSpec as P


def toeplitz(pattern_row, span, window, tap_count):
    pattern = jnp.concatenate([pattern_row, jnp.zeros((window + 1 - tap_count,), jnp.float32)])
    return jnp.tile(pattern, span)[: span * window].reshape(span, window)


def range_filter(block_data, filter_taps):
    gate_count = block_data.shape[3]
    tap_count = filter_taps.shape[1]
    span = min(512, gate_count)
    blocks = gate_count // span
    extent = 1 + (tap_count + span - 2) // span
    window = extent * span
    padded = jnp.pad(block_data, ((0, 0), (0, 0), (0, 0), (0, (extent - 1) * span)))
    shaped = padded.reshape(block_data.shape[:3] + (blocks + extent - 1, span))
    windows = jnp.concatenate(
        [shaped[:, :, :, offset : offset + blocks, :] for offset in range(extent)], axis=4
    )
    toep_re = toeplitz(filter_taps[0], span, window, tap_count)
    toep_im = toeplitz(filter_taps[1], span, window, tap_count)
    joined = jnp.concatenate([windows[0], windows[1]], axis=3)
    table_re = jnp.concatenate([toep_re, -toep_im], axis=1)
    table_im = jnp.concatenate([toep_im, toep_re], axis=1)
    both_tables = jnp.stack([table_re, table_im])
    result = jnp.einsum(
        "abnw,sow->sabno",
        joined,
        both_tables,
        precision=lax.Precision.HIGHEST,
        preferred_element_type=jnp.float32,
    )
    return result.reshape(block_data.shape)


def doppler(block_data):
    pulse_count = block_data.shape[2]
    pulse_idx = jnp.arange(pulse_count, dtype=jnp.int32)
    phases = (pulse_idx[:, None] * pulse_idx[None, :] % pulse_count).astype(jnp.float32) * (
        2.0 * math.pi / pulse_count
    )
    cos_table = jnp.cos(phases)
    sin_table = jnp.sin(phases)
    norm_factor = 1.0 / math.sqrt(pulse_count)

    def contract(part_data, table):
        return jnp.einsum(
            "cpg,pd->cdg",
            part_data,
            table,
            precision=lax.Precision.HIGHEST,
            preferred_element_type=jnp.float32,
        )

    spec_re = (
        contract(block_data[0], cos_table) + contract(block_data[1], sin_table)
    ) * norm_factor
    spec_im = (
        contract(block_data[1], cos_table) - contract(block_data[0], sin_table)
    ) * norm_factor
    return jnp.stack([spec_re, spec_im])


def products(left_part, right_part):
    return jnp.einsum(
        "akg,bkg->kab",
        left_part,
        right_part,
        precision=lax.Precision.HIGHEST,
        preferred_element_type=jnp.float32,
    )


def by_gates(echoes, filter_taps):
    rng_count = lax.axis_size("rng")
    gate_count = echoes.shape[3] * rng_count
    by_bins = lax.all_to_all(doppler(echoes), "rng", split_axis=2, concat_axis=3, tiled=True)
    filtered = range_filter(by_bins, filter_taps)
    gathered = lax.all_to_all(filtered, "chan", split_axis=3, concat_axis=1, tiled=True)
    spec_re = gathered[0]
    spec_im = gathered[1]
    joined = jnp.concatenate([spec_re, spec_im], axis=2)
    turned = jnp.concatenate([spec_im, -spec_re], axis=2)
    real_part = products(joined, joined) / gate_count
    imag_part = products(turned, joined) / gate_count
    summed = (
        lax.psum_scatter(real_part, "chan", scatter_dimension=1, tiled=True),
        lax.psum_scatter(imag_part, "chan", scatter_dimension=1, tiled=True),
    )
    return jnp.stack([summed[0], summed[1]])


def doppler_table(pulse_count):
    idx = jnp.arange(pulse_count, dtype=jnp.int32)
    phases = (idx[:, None] * idx[None, :] % pulse_count).astype(jnp.float32) * (
        2.0 * math.pi / pulse_count
    )
    norm_factor = 1.0 / math.sqrt(pulse_count)
    cos_table = jnp.cos(phases) * norm_factor
    sin_table = jnp.sin(phases) * norm_factor
    return jnp.stack(
        [jnp.stack([cos_table, sin_table]), jnp.stack([-sin_table, cos_table])]
    )


def by_bins(echoes, filter_taps):
    rng_count = lax.axis_size("rng")
    chan_count = lax.axis_size("chan")
    channels, pulse_count, part = echoes.shape[1:]
    gate_count = part * rng_count
    tap_count = filter_taps.shape[1]
    own = pulse_count // (rng_count * chan_count)
    table = doppler_table(pulse_count)
    spectrum = jnp.einsum(
        "tspd,scpg->dtcg",
        table,
        echoes,
        precision=lax.Precision.HIGH,
        preferred_element_type=jnp.float32,
    )
    arrived = lax.all_to_all(spectrum, ("rng", "chan"), split_axis=0, concat_axis=0, tiled=True)
    arrived = arrived.reshape(rng_count, chan_count, own, 2, channels, part)
    samples = arrived.transpose(2, 1, 4, 3, 0, 5).reshape(
        own, chan_count * channels, 2, gate_count
    )
    span = gate_count // 2
    window = gate_count
    toep_re = toeplitz(filter_taps[0], span, window, tap_count).T
    toep_im = toeplitz(filter_taps[1], span, window, tap_count).T
    weights = jnp.stack(
        [jnp.stack([toep_re, toep_im]), jnp.stack([-toep_im, toep_re])]
    )

    def convolve(data, tables):
        return jnp.einsum(
            "bctg,tugx->bcux",
            data,
            tables,
            precision=lax.Precision.HIGH,
            preferred_element_type=jnp.float32,
        )

    halves = [
        convolve(samples, weights),
        convolve(samples[..., span:], weights[:, :, :span]),
    ]

    def correlate(left_part, right_part):
        return jnp.einsum(
            "bag,bcg->bac",
            left_part,
            right_part,
            precision=lax.Precision.HIGH,
            preferred_element_type=jnp.float32,
        )

    real_part = 0.0
    cross = 0.0
    for half in halves:
        flat = half.reshape(own, chan_count * channels, 2 * span)
        real_part = real_part + correlate(flat, flat)
        cross = cross + correlate(half[:, :, 1], half[:, :, 0])
    imag_part = cross - cross.transpose(0, 2, 1)
    both = jnp.stack([real_part, imag_part]) / gate_count
    return lax.all_to_all(both, "chan", split_axis=2, concat_axis=1, tiled=True)


def solution(mesh):
    devices = mesh.shape["rng"] * mesh.shape["chan"]

    def per_device(echoes, filter_taps):
        gate_count = echoes.shape[3] * mesh.shape["rng"]
        whole_bins = echoes.shape[2] % devices == 0
        if whole_bins and gate_count == 2 * filter_taps.shape[1]:
            return by_bins(echoes, filter_taps)
        return by_gates(echoes, filter_taps)

    in_specs = (P(None, "chan", None, "rng"), P())
    out_specs = P(None, "rng", "chan", None)
    return jax.shard_map(
        per_device, mesh=mesh, in_specs=in_specs, out_specs=out_specs, check_vma=False
    )
```

```python
import functools
import math

import jax
import jax.numpy as jnp
import ml_dtypes
import numpy as np
from jax import lax
from jax.experimental import pallas as pl
from jax.experimental.pallas import tpu as pltpu
from jax.sharding import PartitionSpec as P


def toeplitz(pattern_row, span, window, tap_count):
    pattern = jnp.concatenate([pattern_row, jnp.zeros((window + 1 - tap_count,), jnp.float32)])
    return jnp.tile(pattern, span)[: span * window].reshape(span, window)


def range_filter(block_data, filter_taps):
    gate_count = block_data.shape[3]
    tap_count = filter_taps.shape[1]
    span = min(512, gate_count)
    blocks = gate_count // span
    extent = 1 + (tap_count + span - 2) // span
    window = extent * span
    padded = jnp.pad(block_data, ((0, 0), (0, 0), (0, 0), (0, (extent - 1) * span)))
    shaped = padded.reshape(block_data.shape[:3] + (blocks + extent - 1, span))
    windows = jnp.concatenate(
        [shaped[:, :, :, offset : offset + blocks, :] for offset in range(extent)], axis=4
    )
    toep_re = toeplitz(filter_taps[0], span, window, tap_count)
    toep_im = toeplitz(filter_taps[1], span, window, tap_count)
    joined = jnp.concatenate([windows[0], windows[1]], axis=3)
    table_re = jnp.concatenate([toep_re, -toep_im], axis=1)
    table_im = jnp.concatenate([toep_im, toep_re], axis=1)
    both_tables = jnp.stack([table_re, table_im])
    result = jnp.einsum(
        "abnw,sow->sabno",
        joined,
        both_tables,
        precision=lax.Precision.HIGHEST,
        preferred_element_type=jnp.float32,
    )
    return result.reshape(block_data.shape)


def doppler(block_data):
    pulse_count = block_data.shape[2]
    pulse_idx = jnp.arange(pulse_count, dtype=jnp.int32)
    phases = (pulse_idx[:, None] * pulse_idx[None, :] % pulse_count).astype(jnp.float32) * (
        2.0 * math.pi / pulse_count
    )
    cos_table = jnp.cos(phases)
    sin_table = jnp.sin(phases)
    norm_factor = 1.0 / math.sqrt(pulse_count)

    def contract(part_data, table):
        return jnp.einsum(
            "cpg,pd->cdg",
            part_data,
            table,
            precision=lax.Precision.HIGHEST,
            preferred_element_type=jnp.float32,
        )

    spec_re = (
        contract(block_data[0], cos_table) + contract(block_data[1], sin_table)
    ) * norm_factor
    spec_im = (
        contract(block_data[1], cos_table) - contract(block_data[0], sin_table)
    ) * norm_factor
    return jnp.stack([spec_re, spec_im])


def products(left_part, right_part):
    return jnp.einsum(
        "akg,bkg->kab",
        left_part,
        right_part,
        precision=lax.Precision.HIGHEST,
        preferred_element_type=jnp.float32,
    )


def by_gates(echoes, filter_taps):
    rng_count = lax.axis_size("rng")
    gate_count = echoes.shape[3] * rng_count
    by_bins = lax.all_to_all(doppler(echoes), "rng", split_axis=2, concat_axis=3, tiled=True)
    filtered = range_filter(by_bins, filter_taps)
    gathered = lax.all_to_all(filtered, "chan", split_axis=3, concat_axis=1, tiled=True)
    spec_re = gathered[0]
    spec_im = gathered[1]
    joined = jnp.concatenate([spec_re, spec_im], axis=2)
    turned = jnp.concatenate([spec_im, -spec_re], axis=2)
    real_part = products(joined, joined) / gate_count
    imag_part = products(turned, joined) / gate_count
    summed = (
        lax.psum_scatter(real_part, "chan", scatter_dimension=1, tiled=True),
        lax.psum_scatter(imag_part, "chan", scatter_dimension=1, tiled=True),
    )
    return jnp.stack([summed[0], summed[1]])


SPAN = 256
LANES = 128
PIECES = 2
MIB = 2**20


def doppler_table(pulse_count):
    idx = np.arange(pulse_count)
    phases = 2.0 * np.pi * (idx[:, None] * idx[None, :] % pulse_count) / pulse_count
    cos_table = np.cos(phases) / math.sqrt(pulse_count)
    sin_table = np.sin(phases) / math.sqrt(pulse_count)
    rows = np.stack(
        [
            np.concatenate([cos_table, sin_table], axis=1),
            np.concatenate([-sin_table, cos_table], axis=1),
        ],
        axis=1,
    )
    table = rows.reshape(2 * pulse_count, 2 * pulse_count).astype(np.float32)
    high = table.astype(ml_dtypes.bfloat16)
    low = (table - high.astype(np.float32)).astype(ml_dtypes.bfloat16)
    return np.concatenate([high, low, high], axis=1)


def halves_of(values):
    high = values.astype(jnp.bfloat16)
    low = (values - high.astype(jnp.float32)).astype(jnp.bfloat16)
    return high, low


def dot_rows(left, right):
    return lax.dot_general(
        left, right, (((1,), (1,)), ((), ())), preferred_element_type=jnp.float32
    )


def band_kernel(taps_ref, high_ref, low_ref):
    tap_count = taps_ref.shape[1]
    width = tap_count + SPAN
    bands = []
    for part in range(2):
        row = jnp.concatenate(
            [taps_ref[part : part + 1, :], jnp.zeros((1, 2 * SPAN), jnp.float32)], axis=1
        )
        spread = jnp.broadcast_to(row, (SPAN, tap_count + 2 * SPAN))
        bands.append(pltpu.roll(spread, 0, 1, stride=1, stride_axis=0)[:, :width])
    real, imag = bands
    for source, target, band in ((0, 0, real), (0, 1, imag), (1, 0, -imag), (1, 1, real)):
        high, low = halves_of(band)
        high_ref[source, target * SPAN : (target + 1) * SPAN, :] = high
        low_ref[source, target * SPAN : (target + 1) * SPAN, :] = low


def band_tables(filter_taps):
    shape = (2, 2 * SPAN, filter_taps.shape[1] + SPAN)
    return pl.pallas_call(
        band_kernel,
        out_shape=[jax.ShapeDtypeStruct(shape, jnp.bfloat16)] * 2,
        in_specs=[pl.BlockSpec(memory_space=pltpu.VMEM)],
        out_specs=[pl.BlockSpec(memory_space=pltpu.VMEM)] * 2,
        compiler_params=pltpu.CompilerParams(vmem_limit_bytes=32 * MIB),
    )(filter_taps)


def dwell_kernel(
    sizes,
    echoes_ref,
    table_ref,
    band_high,
    band_low,
    out_ref,
    staged,
    outgoing,
    arrived,
    high_ref,
    low_ref,
    rows_ref,
    load_sem,
    send_sem,
    recv_sem,
    row_send_sem,
    row_recv_sem,
):
    rng_count, chan_count, own, channels, pulses, gates = sizes
    devices = rng_count * chan_count
    piece = channels // PIECES
    block = 2 * piece
    my_chan = lax.axis_index("chan")
    my_rng = lax.axis_index("rng")
    me = my_rng * chan_count + my_chan

    def load(part):
        return pltpu.make_async_copy(
            echoes_ref.at[:, pl.ds(part * piece, piece)],
            staged.at[:, pl.ds(part * piece, piece)],
            load_sem.at[part],
        )

    for part in range(PIECES):
        load(part).start()

    barrier = pltpu.get_barrier_semaphore()

    @pl.loop(1, devices)
    def _(step):
        other = lax.rem(me + step, devices)
        pl.semaphore_signal(
            barrier,
            inc=1,
            device_id={"chan": lax.rem(other, chan_count), "rng": other // chan_count},
            device_id_type=pl.DeviceIdType.MESH,
        )

    def chunk(part, bin_index):
        return outgoing.at[pl.ds((part * pulses + bin_index) * block, block)]

    def send(part, slot):
        @pl.loop(0, devices - 1)
        def _(step):
            offset = devices // 2 + step
            offset = offset + (offset >= devices).astype(jnp.int32)
            other = lax.rem(me + offset, devices)
            pltpu.make_async_remote_copy(
                src_ref=chunk(part, other * own + slot),
                dst_ref=arrived.at[slot, part, my_rng, my_chan],
                send_sem=send_sem.at[part],
                recv_sem=recv_sem.at[slot, part],
                device_id={"chan": lax.rem(other, chan_count), "rng": other // chan_count},
                device_id_type=pl.DeviceIdType.MESH,
            ).start()

        pltpu.make_async_copy(
            chunk(part, me * own + slot),
            arrived.at[slot, part, my_rng, my_chan],
            recv_sem.at[slot, part],
        ).start()

    for part in range(PIECES):
        load(part).wait()

        @pl.loop(0, piece // 8)
        def _(group):
            columns = []
            for lane in range(8):
                channel = part * piece + group * 8 + lane
                columns.append(
                    jnp.concatenate([staged[0, channel], staged[1, channel]], axis=0)
                )
            high, low = halves_of(jnp.concatenate(columns, axis=1))
            spectrum = jnp.dot(
                table_ref[...],
                jnp.concatenate([high, high, low], axis=0),
                preferred_element_type=jnp.float32,
            )
            for lane in range(8):
                first = part * pulses * block + group * 8 + lane
                outgoing[pl.ds(first, 2 * pulses, stride=piece), :] = spectrum[
                    :, lane * LANES : (lane + 1) * LANES
                ]

        if part == 0:
            pl.semaphore_wait(barrier, devices - 1)
        send(part, 0)
    for slot in range(1, own):
        for part in range(PIECES):
            send(part, slot)

    spans = gates // SPAN
    reach = band_high.shape[2] // SPAN
    per_span = SPAN // LANES

    def finish(slot):
        @pl.loop(0, PIECES)
        def _(part):
            pltpu.make_async_copy(
                arrived.at[slot, part], arrived.at[slot, part], recv_sem.at[slot, part]
            ).wait()

            def samples(source, first):
                columns = []
                for rng in range(first * per_span, (first + 1) * per_span):
                    tile = arrived[slot, part, rng, :, pl.ds(source * piece, piece), :]
                    columns.append(tile.reshape(chan_count * piece, LANES))
                return halves_of(jnp.concatenate(columns, axis=1))

            pairs = [[samples(source, first) for first in range(spans)] for source in range(2)]
            for target in range(spans):
                count = min(reach, spans - target)
                total = jnp.zeros((chan_count * piece, 2 * SPAN), jnp.float32)
                for source in range(2):
                    taken = pairs[source][target : target + count]
                    high = jnp.concatenate([pair[0] for pair in taken], axis=1)
                    low = jnp.concatenate([pair[1] for pair in taken], axis=1)
                    width = count * SPAN
                    total = total + dot_rows(high, band_high[source, :, :width])
                    total = total + dot_rows(high, band_low[source, :, :width])
                    total = total + dot_rows(low, band_high[source, :, :width])
                high, low = halves_of(total)
                for chan in range(chan_count):
                    rows = pl.ds(
                        pl.multiple_of(chan * channels + part * piece, piece), piece
                    )
                    local = slice(chan * piece, (chan + 1) * piece)
                    for side in range(2):
                        start = side * gates + target * SPAN
                        span_cols = slice(side * SPAN, (side + 1) * SPAN)
                        high_ref[rows, start : start + SPAN] = high[local, span_cols]
                        low_ref[rows, start : start + SPAN] = low[local, span_cols]

        half = chan_count // 2

        @pl.loop(0, chan_count)
        def _(step):
            offset = jnp.where(step < half, half + step, chan_count - 1 - step)
            owner = lax.rem(my_chan + offset, chan_count)
            rows = pl.ds(pl.multiple_of(owner * channels, channels), channels)

            def outer(left, right):
                lefts = slice(left * gates, (left + 1) * gates)
                rights = slice(right * gates, (right + 1) * gates)
                total = dot_rows(high_ref[rows, lefts], high_ref[:, rights])
                total = total + dot_rows(high_ref[rows, lefts], low_ref[:, rights])
                return total + dot_rows(low_ref[rows, lefts], high_ref[:, rights])

            rows_ref[slot, owner, 0] = (outer(0, 0) + outer(1, 1)) * (1.0 / gates)
            rows_ref[slot, owner, 1] = (outer(1, 0) - outer(0, 1)) * (1.0 / gates)
            target_ref = out_ref.at[:, my_chan * own + slot]

            @pl.when(owner != my_chan)
            def _():
                pltpu.make_async_remote_copy(
                    src_ref=rows_ref.at[slot, owner],
                    dst_ref=target_ref,
                    send_sem=row_send_sem.at[slot],
                    recv_sem=row_recv_sem.at[slot],
                    device_id={"chan": owner, "rng": my_rng},
                    device_id_type=pl.DeviceIdType.MESH,
                ).start()

            @pl.when(owner == my_chan)
            def _():
                pltpu.make_async_copy(
                    rows_ref.at[slot, owner], target_ref, row_recv_sem.at[slot]
                ).start()

    @pl.loop(0, own)
    def _(slot):
        finish(slot)

    for part in range(PIECES):
        sent = outgoing.at[pl.ds(0, (pulses - own) * block)]
        pltpu.make_async_copy(sent, sent, send_sem.at[part]).wait()
    for slot in range(own):
        given = rows_ref.at[slot, pl.ds(0, chan_count - 1)]
        pltpu.make_async_copy(given, given, row_send_sem.at[slot]).wait()
        taken = out_ref.at[:, pl.ds(0, chan_count)]
        pltpu.make_async_copy(taken, taken, row_recv_sem.at[slot]).wait()


def by_bins(echoes, filter_taps, rng_count, chan_count):
    channels, pulses, part = echoes.shape[1:]
    gates = part * rng_count
    own = pulses // (rng_count * chan_count)
    piece = channels // PIECES
    whole = channels * chan_count
    sizes = (rng_count, chan_count, own, channels, pulses, gates)
    band_high, band_low = band_tables(filter_taps)
    vmem = pl.BlockSpec(memory_space=pltpu.VMEM)
    hbm = pl.BlockSpec(memory_space=pl.ANY)
    return pl.pallas_call(
        functools.partial(dwell_kernel, sizes),
        out_shape=jax.ShapeDtypeStruct((2, own * chan_count, channels, whole), jnp.float32),
        in_specs=[hbm, vmem, vmem, vmem],
        out_specs=hbm,
        scratch_shapes=[
            pltpu.VMEM(echoes.shape, jnp.float32),
            pltpu.VMEM((2 * pulses * channels, part), jnp.float32),
            pltpu.VMEM((own, PIECES, rng_count, chan_count, 2 * piece, part), jnp.float32),
            pltpu.VMEM((whole, 2 * gates), jnp.bfloat16),
            pltpu.VMEM((whole, 2 * gates), jnp.bfloat16),
            pltpu.VMEM((own, chan_count, 2, channels, whole), jnp.float32),
            pltpu.SemaphoreType.DMA((PIECES,)),
            pltpu.SemaphoreType.DMA((PIECES,)),
            pltpu.SemaphoreType.DMA((own, PIECES)),
            pltpu.SemaphoreType.DMA((own,)),
            pltpu.SemaphoreType.DMA((own,)),
        ],
        compiler_params=pltpu.CompilerParams(
            collective_id=0, has_side_effects=True, vmem_limit_bytes=56 * MIB
        ),
    )(echoes, jnp.asarray(doppler_table(pulses)), band_high, band_low)


def solution(mesh):
    rng_count = mesh.shape["rng"]
    chan_count = mesh.shape["chan"]

    def per_device(echoes, filter_taps):
        channels, pulses, part = echoes.shape[1:]
        fits = (
            pulses % (rng_count * chan_count) == 0
            and part == LANES
            and (part * rng_count) % SPAN == 0
            and filter_taps.shape[1] % SPAN == 0
            and channels % (16 * PIECES) == 0
        )
        if fits:
            return by_bins(echoes, filter_taps, rng_count, chan_count)
        return by_gates(echoes, filter_taps)

    in_specs = (P(None, "chan", None, "rng"), P())
    out_specs = P(None, "rng", "chan", None)
    return jax.shard_map(
        per_device, mesh=mesh, in_specs=in_specs, out_specs=out_specs, check_vma=False
    )
```

```python
import functools
import math

import jax
import jax.numpy as jnp
import ml_dtypes
import numpy as np
from jax import lax
from jax.experimental import pallas as pl
from jax.experimental.pallas import tpu as pltpu
from jax.sharding import PartitionSpec as P


def toeplitz(pattern_row, span, window, tap_count):
    pattern = jnp.concatenate([pattern_row, jnp.zeros((window + 1 - tap_count,), jnp.float32)])
    return jnp.tile(pattern, span)[: span * window].reshape(span, window)


def range_filter(block_data, filter_taps):
    gate_count = block_data.shape[3]
    tap_count = filter_taps.shape[1]
    span = min(512, gate_count)
    blocks = gate_count // span
    extent = 1 + (tap_count + span - 2) // span
    window = extent * span
    padded = jnp.pad(block_data, ((0, 0), (0, 0), (0, 0), (0, (extent - 1) * span)))
    shaped = padded.reshape(block_data.shape[:3] + (blocks + extent - 1, span))
    windows = jnp.concatenate(
        [shaped[:, :, :, offset : offset + blocks, :] for offset in range(extent)], axis=4
    )
    toep_re = toeplitz(filter_taps[0], span, window, tap_count)
    toep_im = toeplitz(filter_taps[1], span, window, tap_count)
    joined = jnp.concatenate([windows[0], windows[1]], axis=3)
    table_re = jnp.concatenate([toep_re, -toep_im], axis=1)
    table_im = jnp.concatenate([toep_im, toep_re], axis=1)
    both_tables = jnp.stack([table_re, table_im])
    result = jnp.einsum(
        "abnw,sow->sabno",
        joined,
        both_tables,
        precision=lax.Precision.HIGHEST,
        preferred_element_type=jnp.float32,
    )
    return result.reshape(block_data.shape)


def doppler(block_data):
    pulse_count = block_data.shape[2]
    pulse_idx = jnp.arange(pulse_count, dtype=jnp.int32)
    phases = (pulse_idx[:, None] * pulse_idx[None, :] % pulse_count).astype(jnp.float32) * (
        2.0 * math.pi / pulse_count
    )
    cos_table = jnp.cos(phases)
    sin_table = jnp.sin(phases)
    norm_factor = 1.0 / math.sqrt(pulse_count)

    def contract(part_data, table):
        return jnp.einsum(
            "cpg,pd->cdg",
            part_data,
            table,
            precision=lax.Precision.HIGHEST,
            preferred_element_type=jnp.float32,
        )

    spec_re = (
        contract(block_data[0], cos_table) + contract(block_data[1], sin_table)
    ) * norm_factor
    spec_im = (
        contract(block_data[1], cos_table) - contract(block_data[0], sin_table)
    ) * norm_factor
    return jnp.stack([spec_re, spec_im])


def products(left_part, right_part):
    return jnp.einsum(
        "akg,bkg->kab",
        left_part,
        right_part,
        precision=lax.Precision.HIGHEST,
        preferred_element_type=jnp.float32,
    )


def by_gates(echoes, filter_taps):
    rng_count = lax.axis_size("rng")
    gate_count = echoes.shape[3] * rng_count
    by_bins = lax.all_to_all(doppler(echoes), "rng", split_axis=2, concat_axis=3, tiled=True)
    filtered = range_filter(by_bins, filter_taps)
    gathered = lax.all_to_all(filtered, "chan", split_axis=3, concat_axis=1, tiled=True)
    spec_re = gathered[0]
    spec_im = gathered[1]
    joined = jnp.concatenate([spec_re, spec_im], axis=2)
    turned = jnp.concatenate([spec_im, -spec_re], axis=2)
    real_part = products(joined, joined) / gate_count
    imag_part = products(turned, joined) / gate_count
    summed = (
        lax.psum_scatter(real_part, "chan", scatter_dimension=1, tiled=True),
        lax.psum_scatter(imag_part, "chan", scatter_dimension=1, tiled=True),
    )
    return jnp.stack([summed[0], summed[1]])


SPAN = 256
LANES = 128
SUBS = 4
MIB = 2**20


def doppler_table(pulse_count):
    idx = np.arange(pulse_count)
    phases = 2.0 * np.pi * (idx[:, None] * idx[None, :] % pulse_count) / pulse_count
    cos_table = np.cos(phases) / math.sqrt(pulse_count)
    sin_table = np.sin(phases) / math.sqrt(pulse_count)
    rows = np.stack(
        [
            np.concatenate([cos_table, sin_table], axis=1),
            np.concatenate([-sin_table, cos_table], axis=1),
        ],
        axis=0,
    )
    table = rows.reshape(2 * pulse_count, 2 * pulse_count).astype(np.float32)
    high = table.astype(ml_dtypes.bfloat16)
    low = (table - high.astype(np.float32)).astype(ml_dtypes.bfloat16)
    return np.concatenate([high, low, high], axis=1)


def halves_of(values):
    high = values.astype(jnp.bfloat16)
    low = (values - high.astype(jnp.float32)).astype(jnp.bfloat16)
    return high, low


def dot_rows(left, right):
    return lax.dot_general(
        left, right, (((1,), (1,)), ((), ())), preferred_element_type=jnp.float32
    )


def band_kernel(taps_ref, high_ref, low_ref):
    tap_count = taps_ref.shape[1]
    width = tap_count + SPAN
    bands = []
    for part in range(2):
        row = jnp.concatenate(
            [taps_ref[part : part + 1, :], jnp.zeros((1, 2 * SPAN), jnp.float32)], axis=1
        )
        spread = jnp.broadcast_to(row, (SPAN, tap_count + 2 * SPAN))
        bands.append(pltpu.roll(spread, 0, 1, stride=1, stride_axis=0)[:, :width])
    real, imag = bands
    for source, target, band in ((0, 0, real), (0, 1, imag), (1, 0, -imag), (1, 1, real)):
        high, low = halves_of(band)
        high_ref[source, target * SPAN : (target + 1) * SPAN, :] = high
        low_ref[source, target * SPAN : (target + 1) * SPAN, :] = low


def band_tables(filter_taps):
    shape = (2, 2 * SPAN, filter_taps.shape[1] + SPAN)
    return pl.pallas_call(
        band_kernel,
        out_shape=[jax.ShapeDtypeStruct(shape, jnp.bfloat16)] * 2,
        in_specs=[pl.BlockSpec(memory_space=pltpu.VMEM)],
        out_specs=[pl.BlockSpec(memory_space=pltpu.VMEM)] * 2,
        compiler_params=pltpu.CompilerParams(vmem_limit_bytes=32 * MIB),
    )(filter_taps)


def dwell_kernel(
    sizes,
    echoes_ref,
    table_ref,
    band_high,
    band_low,
    out_ref,
    staged,
    outgoing,
    arrived,
    high_ref,
    low_ref,
    rows_ref,
    early_ref,
    edge_ref,
    late_ref,
    load_sem,
    send_sem,
    recv_sem,
    row_send_sem,
    row_recv_sem,
    early_sem,
    late_sem,
):
    rng_count, chan_count, own, channels, pulses, gates = sizes
    devices = rng_count * chan_count
    small = channels // SUBS
    big = channels - small
    pieces = ((0, small), (small, big))
    last = own - 1
    my_chan = lax.axis_index("chan")
    my_rng = lax.axis_index("rng")
    me = my_rng * chan_count + my_chan

    def load(index):
        first, count = pieces[index]
        return pltpu.make_async_copy(
            echoes_ref.at[:, pl.ds(first, count)],
            staged.at[:, pl.ds(first, count)],
            load_sem.at[index],
        )

    for index in range(2):
        load(index).start()

    barrier = pltpu.get_barrier_semaphore()

    @pl.loop(1, devices)
    def _(step):
        other = lax.rem(me + step, devices)
        pl.semaphore_signal(
            barrier,
            inc=1,
            device_id={"chan": lax.rem(other, chan_count), "rng": other // chan_count},
            device_id_type=pl.DeviceIdType.MESH,
        )

    def chunk(index, bin_index):
        first, count = pieces[index]
        return outgoing.at[pl.ds(2 * (first * pulses + bin_index * count), 2 * count)]

    def landing(index, slot):
        first, count = pieces[index]
        return arrived.at[slot, my_rng, my_chan, pl.ds(2 * first, 2 * count)]

    def send(index, slot):
        @pl.loop(0, devices - 1)
        def _(step):
            offset = devices // 2 + step
            offset = offset + (offset >= devices).astype(jnp.int32)
            other = lax.rem(me + offset, devices)
            pltpu.make_async_remote_copy(
                src_ref=chunk(index, other * own + slot),
                dst_ref=landing(index, slot),
                send_sem=send_sem.at[index],
                recv_sem=recv_sem.at[slot, index],
                device_id={"chan": lax.rem(other, chan_count), "rng": other // chan_count},
                device_id_type=pl.DeviceIdType.MESH,
            ).start()

        pltpu.make_async_copy(
            chunk(index, me * own + slot), landing(index, slot), recv_sem.at[slot, index]
        ).start()

    def transform(index):
        first, count = pieces[index]

        @pl.loop(0, count // 8)
        def _(group):
            columns = []
            for lane in range(8):
                channel = first + group * 8 + lane
                columns.append(
                    jnp.concatenate([staged[0, channel], staged[1, channel]], axis=0)
                )
            high, low = halves_of(jnp.concatenate(columns, axis=1))
            spectrum = jnp.dot(
                table_ref[...],
                jnp.concatenate([high, high, low], axis=0),
                preferred_element_type=jnp.float32,
            )
            sub = group // (small // 8)
            place = sub * 2 * small + (group - sub * (small // 8)) * 8
            for side in range(2):
                for lane in range(8):
                    start = 2 * first * pulses + side * small + place + lane
                    outgoing[pl.ds(start, pulses, stride=2 * count), :] = spectrum[
                        side * pulses : (side + 1) * pulses,
                        lane * LANES : (lane + 1) * LANES,
                    ]

    for index in range(2):
        load(index).wait()
        transform(index)
        if index == 0:
            pl.semaphore_wait(barrier, devices - 1)
        send(index, 0)
    for slot in range(1, own):
        for index in (1, 0):
            send(index, slot)

    spans = gates // SPAN
    reach = band_high.shape[2] // SPAN
    per_span = SPAN // LANES

    def receive(index, slot):
        first, count = pieces[index]
        landed = arrived.at[slot, :, :, pl.ds(2 * first, 2 * count)]
        pltpu.make_async_copy(landed, landed, recv_sem.at[slot, index]).wait()

    def convolve(sub, slot):
        def samples(source, first):
            columns = []
            for rng in range(first * per_span, (first + 1) * per_span):
                rows = pl.ds(pl.multiple_of((2 * sub + source) * small, small), small)
                tile = arrived[slot, rng, :, rows, :]
                columns.append(tile.reshape(chan_count * small, LANES))
            return halves_of(jnp.concatenate(columns, axis=1))

        pairs = [[samples(source, first) for first in range(spans)] for source in range(2)]
        for target in range(spans):
            count = min(reach, spans - target)
            total = jnp.zeros((chan_count * small, 2 * SPAN), jnp.float32)
            for source in range(2):
                taken = pairs[source][target : target + count]
                high = jnp.concatenate([pair[0] for pair in taken], axis=1)
                low = jnp.concatenate([pair[1] for pair in taken], axis=1)
                width = count * SPAN
                total = total + dot_rows(high, band_high[source, :, :width])
                total = total + dot_rows(high, band_low[source, :, :width])
                total = total + dot_rows(low, band_high[source, :, :width])
            high, low = halves_of(total)
            for chan in range(chan_count):
                rows = pl.ds(pl.multiple_of(chan * channels + sub * small, small), small)
                local = slice(chan * small, (chan + 1) * small)
                for side in range(2):
                    start = side * gates + target * SPAN
                    span_cols = slice(side * SPAN, (side + 1) * SPAN)
                    high_ref[rows, start : start + SPAN] = high[local, span_cols]
                    low_ref[rows, start : start + SPAN] = low[local, span_cols]

    def outer(left, right):
        def one(first, second):
            lefts = slice(first * gates, (first + 1) * gates)
            rights = slice(second * gates, (second + 1) * gates)
            total = dot_rows(left[0](lefts), right[0](rights))
            total = total + dot_rows(left[0](lefts), right[1](rights))
            return total + dot_rows(left[1](lefts), right[0](rights))

        scale = 1.0 / gates
        return (one(0, 0) + one(1, 1)) * scale, (one(1, 0) - one(0, 1)) * scale

    def rows_of(first, count):
        rows = pl.ds(pl.multiple_of(first, small), count)
        return tuple(lambda cols, ref=ref: ref[rows, cols] for ref in (high_ref, low_ref))

    every = tuple(lambda cols, ref=ref: ref[:, cols] for ref in (high_ref, low_ref))

    def edge(cols, ref):
        return jnp.concatenate(
            [ref[chan * channels : chan * channels + small, cols] for chan in range(chan_count)],
            axis=0,
        )

    edges = tuple(lambda cols, ref=ref: edge(cols, ref) for ref in (high_ref, low_ref))

    def owner_at(step):
        half = chan_count // 2
        offset = jnp.where(step < half, half + step, chan_count - 1 - step)
        return lax.rem(my_chan + offset, chan_count)

    def hand_over(owner, source, target, send_to, recv_from):
        @pl.when(owner != my_chan)
        def _():
            pltpu.make_async_remote_copy(
                src_ref=source,
                dst_ref=target,
                send_sem=send_to,
                recv_sem=recv_from,
                device_id={"chan": owner, "rng": my_rng},
                device_id_type=pl.DeviceIdType.MESH,
            ).start()

        @pl.when(owner == my_chan)
        def _():
            pltpu.make_async_copy(source, target, recv_from).start()

    for slot in range(last):
        receive(0, slot)
        convolve(0, slot)
        receive(1, slot)

        @pl.loop(1, SUBS)
        def _(sub):
            convolve(sub, slot)

        @pl.loop(0, chan_count)
        def _(step):
            owner = owner_at(step)
            real, imag = outer(rows_of(owner * channels, channels), every)
            rows_ref[slot, owner, 0] = real
            rows_ref[slot, owner, 1] = imag
            hand_over(
                owner,
                rows_ref.at[slot, owner],
                out_ref.at[:, my_chan * own + slot],
                row_send_sem.at[slot],
                row_recv_sem.at[slot],
            )

    receive(1, last)

    @pl.loop(1, SUBS)
    def _(sub):
        convolve(sub, last)

    @pl.loop(0, chan_count)
    def _(step):
        owner = owner_at(step)
        real, imag = outer(rows_of(owner * channels + small, big), every)
        rows_ref[last, owner, 0, small:, :] = real
        rows_ref[last, owner, 1, small:, :] = imag
        hand_over(
            owner,
            rows_ref.at[last, owner, :, pl.ds(small, big)],
            early_ref.at[my_chan],
            early_sem.at[0],
            early_sem.at[1],
        )

    receive(0, last)
    convolve(0, last)
    real, imag = outer(edges, every)
    for chan in range(chan_count):
        local = slice(chan * small, (chan + 1) * small)
        rows_ref[last, chan, 0, :small, :] = real[local]
        rows_ref[last, chan, 1, :small, :] = imag[local]

    @pl.loop(0, chan_count)
    def _(step):
        owner = owner_at(step)
        hand_over(
            owner,
            rows_ref.at[last, owner, :, pl.ds(0, small)],
            out_ref.at[:, my_chan * own + last, pl.ds(0, small)],
            row_send_sem.at[last],
            row_recv_sem.at[last],
        )

    @pl.loop(0, chan_count)
    def _(step):
        owner = owner_at(step)
        real, imag = outer(rows_of(owner * channels + small, big), edges)
        edge_ref[owner, 0] = real
        edge_ref[owner, 1] = imag
        hand_over(
            owner, edge_ref.at[owner], late_ref.at[my_chan], late_sem.at[0], late_sem.at[1]
        )

    pltpu.make_async_copy(early_ref, early_ref, early_sem.at[1]).wait()
    pltpu.make_async_copy(late_ref, late_ref, late_sem.at[1]).wait()
    width = chan_count * small
    lanes = lax.broadcasted_iota(jnp.int32, (big, width), 1)
    for chan in range(chan_count):
        for side in range(2):
            late = late_ref[chan, side]
            for tile in range(chan_count):
                cols = slice(tile * channels, (tile + 1) * channels)
                moved = pltpu.roll(late, (width - tile * small) % width, 1)
                early_ref[chan, side, :, cols] = jnp.where(
                    lanes < small, moved, early_ref[chan, side, :, cols]
                )

    def deliver(chan):
        return pltpu.make_async_copy(
            early_ref.at[chan],
            out_ref.at[:, chan * own + last, pl.ds(small, big)],
            load_sem.at[chan],
        )

    for chan in range(chan_count):
        deliver(chan).start()
    for index in range(2):
        first, count = pieces[index]
        sent = outgoing.at[pl.ds(0, 2 * (pulses - own) * count)]
        pltpu.make_async_copy(sent, sent, send_sem.at[index]).wait()
    others = pl.ds(0, chan_count - 1)
    bins = pl.ds(0, chan_count)
    for slot in range(last):
        given = rows_ref.at[slot, others]
        pltpu.make_async_copy(given, given, row_send_sem.at[slot]).wait()
        taken = out_ref.at[:, bins]
        pltpu.make_async_copy(taken, taken, row_recv_sem.at[slot]).wait()
    given = rows_ref.at[last, others, :, pl.ds(0, small)]
    pltpu.make_async_copy(given, given, row_send_sem.at[last]).wait()
    taken = out_ref.at[:, bins, pl.ds(0, small)]
    pltpu.make_async_copy(taken, taken, row_recv_sem.at[last]).wait()
    given = early_ref.at[others]
    pltpu.make_async_copy(given, given, early_sem.at[0]).wait()
    given = edge_ref.at[others]
    pltpu.make_async_copy(given, given, late_sem.at[0]).wait()
    for chan in range(chan_count):
        deliver(chan).wait()


def by_bins(echoes, filter_taps, rng_count, chan_count):
    channels, pulses, part = echoes.shape[1:]
    gates = part * rng_count
    own = pulses // (rng_count * chan_count)
    small = channels // SUBS
    big = channels - small
    whole = channels * chan_count
    sizes = (rng_count, chan_count, own, channels, pulses, gates)
    band_high, band_low = band_tables(filter_taps)
    vmem = pl.BlockSpec(memory_space=pltpu.VMEM)
    hbm = pl.BlockSpec(memory_space=pl.ANY)
    return pl.pallas_call(
        functools.partial(dwell_kernel, sizes),
        out_shape=jax.ShapeDtypeStruct((2, own * chan_count, channels, whole), jnp.float32),
        in_specs=[hbm, vmem, vmem, vmem],
        out_specs=hbm,
        scratch_shapes=[
            pltpu.VMEM(echoes.shape, jnp.float32),
            pltpu.VMEM((2 * pulses * channels, part), jnp.float32),
            pltpu.VMEM((own, rng_count, chan_count, 2 * channels, part), jnp.float32),
            pltpu.VMEM((whole, 2 * gates), jnp.bfloat16),
            pltpu.VMEM((whole, 2 * gates), jnp.bfloat16),
            pltpu.VMEM((own, chan_count, 2, channels, whole), jnp.float32),
            pltpu.VMEM((chan_count, 2, big, whole), jnp.float32),
            pltpu.VMEM((chan_count, 2, big, chan_count * small), jnp.float32),
            pltpu.VMEM((chan_count, 2, big, chan_count * small), jnp.float32),
            pltpu.SemaphoreType.DMA((max(2, chan_count),)),
            pltpu.SemaphoreType.DMA((2,)),
            pltpu.SemaphoreType.DMA((own, 2)),
            pltpu.SemaphoreType.DMA((own,)),
            pltpu.SemaphoreType.DMA((own,)),
            pltpu.SemaphoreType.DMA((2,)),
            pltpu.SemaphoreType.DMA((2,)),
        ],
        compiler_params=pltpu.CompilerParams(
            collective_id=0, has_side_effects=True, vmem_limit_bytes=56 * MIB
        ),
    )(echoes, jnp.asarray(doppler_table(pulses)), band_high, band_low)


def solution(mesh):
    rng_count = mesh.shape["rng"]
    chan_count = mesh.shape["chan"]

    def per_device(echoes, filter_taps):
        channels, pulses, part = echoes.shape[1:]
        fits = (
            pulses % (rng_count * chan_count) == 0
            and pulses >= 2 * rng_count * chan_count
            and chan_count == SUBS
            and channels == LANES
            and part == LANES
            and (part * rng_count) % SPAN == 0
            and filter_taps.shape[1] % SPAN == 0
        )
        if fits:
            return by_bins(echoes, filter_taps, rng_count, chan_count)
        return by_gates(echoes, filter_taps)

    in_specs = (P(None, "chan", None, "rng"), P())
    out_specs = P(None, "rng", "chan", None)
    return jax.shard_map(
        per_device, mesh=mesh, in_specs=in_specs, out_specs=out_specs, check_vma=False
    )
```

```python
import functools
import math

import jax
import jax.numpy as jnp
import ml_dtypes
import numpy as np
from jax import lax
from jax.experimental import pallas as pl
from jax.experimental.pallas import tpu as pltpu
from jax.sharding import PartitionSpec as P


def toeplitz(pattern_row, span, window, tap_count):
    pattern = jnp.concatenate([pattern_row, jnp.zeros((window + 1 - tap_count,), jnp.float32)])
    return jnp.tile(pattern, span)[: span * window].reshape(span, window)


def range_filter(block_data, filter_taps):
    gate_count = block_data.shape[3]
    tap_count = filter_taps.shape[1]
    span = min(512, gate_count)
    blocks = gate_count // span
    extent = 1 + (tap_count + span - 2) // span
    window = extent * span
    padded = jnp.pad(block_data, ((0, 0), (0, 0), (0, 0), (0, (extent - 1) * span)))
    shaped = padded.reshape(block_data.shape[:3] + (blocks + extent - 1, span))
    windows = jnp.concatenate(
        [shaped[:, :, :, offset : offset + blocks, :] for offset in range(extent)], axis=4
    )
    toep_re = toeplitz(filter_taps[0], span, window, tap_count)
    toep_im = toeplitz(filter_taps[1], span, window, tap_count)
    joined = jnp.concatenate([windows[0], windows[1]], axis=3)
    table_re = jnp.concatenate([toep_re, -toep_im], axis=1)
    table_im = jnp.concatenate([toep_im, toep_re], axis=1)
    both_tables = jnp.stack([table_re, table_im])
    result = jnp.einsum(
        "abnw,sow->sabno",
        joined,
        both_tables,
        precision=lax.Precision.HIGHEST,
        preferred_element_type=jnp.float32,
    )
    return result.reshape(block_data.shape)


def doppler(block_data):
    pulse_count = block_data.shape[2]
    pulse_idx = jnp.arange(pulse_count, dtype=jnp.int32)
    phases = (pulse_idx[:, None] * pulse_idx[None, :] % pulse_count).astype(jnp.float32) * (
        2.0 * math.pi / pulse_count
    )
    cos_table = jnp.cos(phases)
    sin_table = jnp.sin(phases)
    norm_factor = 1.0 / math.sqrt(pulse_count)

    def contract(part_data, table):
        return jnp.einsum(
            "cpg,pd->cdg",
            part_data,
            table,
            precision=lax.Precision.HIGHEST,
            preferred_element_type=jnp.float32,
        )

    spec_re = (
        contract(block_data[0], cos_table) + contract(block_data[1], sin_table)
    ) * norm_factor
    spec_im = (
        contract(block_data[1], cos_table) - contract(block_data[0], sin_table)
    ) * norm_factor
    return jnp.stack([spec_re, spec_im])


def products(left_part, right_part):
    return jnp.einsum(
        "akg,bkg->kab",
        left_part,
        right_part,
        precision=lax.Precision.HIGHEST,
        preferred_element_type=jnp.float32,
    )


def by_gates(echoes, filter_taps):
    rng_count = lax.axis_size("rng")
    gate_count = echoes.shape[3] * rng_count
    by_bins = lax.all_to_all(doppler(echoes), "rng", split_axis=2, concat_axis=3, tiled=True)
    filtered = range_filter(by_bins, filter_taps)
    gathered = lax.all_to_all(filtered, "chan", split_axis=3, concat_axis=1, tiled=True)
    spec_re = gathered[0]
    spec_im = gathered[1]
    joined = jnp.concatenate([spec_re, spec_im], axis=2)
    turned = jnp.concatenate([spec_im, -spec_re], axis=2)
    real_part = products(joined, joined) / gate_count
    imag_part = products(turned, joined) / gate_count
    summed = (
        lax.psum_scatter(real_part, "chan", scatter_dimension=1, tiled=True),
        lax.psum_scatter(imag_part, "chan", scatter_dimension=1, tiled=True),
    )
    return jnp.stack([summed[0], summed[1]])


SPAN = 256
LANES = 128
SUBS = 4
WINDOW = 3
MIB = 2**20


def doppler_table(pulse_count):
    idx = np.arange(pulse_count)
    phases = 2.0 * np.pi * (idx[:, None] * idx[None, :] % pulse_count) / pulse_count
    cos_table = np.cos(phases) / math.sqrt(pulse_count)
    sin_table = np.sin(phases) / math.sqrt(pulse_count)
    rows = np.stack(
        [
            np.concatenate([cos_table, sin_table], axis=1),
            np.concatenate([-sin_table, cos_table], axis=1),
        ],
        axis=0,
    )
    table = rows.reshape(2 * pulse_count, 2 * pulse_count).astype(np.float32)
    high = table.astype(ml_dtypes.bfloat16)
    low = (table - high.astype(np.float32)).astype(ml_dtypes.bfloat16)
    return np.concatenate([high, low, high], axis=1)


def halves_of(values):
    high = values.astype(jnp.bfloat16)
    low = (values - high.astype(jnp.float32)).astype(jnp.bfloat16)
    return high, low


def dot_rows(left, right):
    return lax.dot_general(
        left, right, (((1,), (1,)), ((), ())), preferred_element_type=jnp.float32
    )


def band_kernel(taps_ref, high_ref, low_ref):
    tap_count = taps_ref.shape[1]
    width = tap_count + SPAN
    bands = []
    for part in range(2):
        row = jnp.concatenate(
            [taps_ref[part : part + 1, :], jnp.zeros((1, 2 * SPAN), jnp.float32)], axis=1
        )
        spread = jnp.broadcast_to(row, (SPAN, tap_count + 2 * SPAN))
        bands.append(pltpu.roll(spread, 0, 1, stride=1, stride_axis=0)[:, :width])
    real, imag = bands
    for source, target, band in ((0, 0, real), (0, 1, imag), (1, 0, -imag), (1, 1, real)):
        high, low = halves_of(band)
        high_ref[source, target * SPAN : (target + 1) * SPAN, :] = high
        low_ref[source, target * SPAN : (target + 1) * SPAN, :] = low


def band_tables(filter_taps):
    shape = (2, 2 * SPAN, filter_taps.shape[1] + SPAN)
    return pl.pallas_call(
        band_kernel,
        out_shape=[jax.ShapeDtypeStruct(shape, jnp.bfloat16)] * 2,
        in_specs=[pl.BlockSpec(memory_space=pltpu.VMEM)],
        out_specs=[pl.BlockSpec(memory_space=pltpu.VMEM)] * 2,
        compiler_params=pltpu.CompilerParams(vmem_limit_bytes=32 * MIB),
    )(filter_taps)


def dwell_kernel(
    sizes,
    echoes_ref,
    table_ref,
    band_high,
    band_low,
    out_ref,
    staged,
    outgoing,
    arrived,
    high_ref,
    low_ref,
    rows_ref,
    early_ref,
    edge_ref,
    late_ref,
    load_sem,
    send_sem,
    recv_sem,
    row_send_sem,
    row_recv_sem,
    early_sem,
    late_sem,
):
    rng_count, chan_count, own, channels, pulses, gates = sizes
    devices = rng_count * chan_count
    small = channels // SUBS
    big = channels - small
    pieces = ((0, small), (small, big))
    last = own - 1
    my_chan = lax.axis_index("chan")
    my_rng = lax.axis_index("rng")
    me = my_rng * chan_count + my_chan

    def load(index):
        first, count = pieces[index]
        return pltpu.make_async_copy(
            echoes_ref.at[:, pl.ds(first, count)],
            staged.at[:, pl.ds(first, count)],
            load_sem.at[index],
        )

    for index in range(2):
        load(index).start()

    barrier = pltpu.get_barrier_semaphore()

    @pl.loop(1, devices)
    def _(step):
        other = lax.rem(me + step, devices)
        pl.semaphore_signal(
            barrier,
            inc=1,
            device_id={"chan": lax.rem(other, chan_count), "rng": other // chan_count},
            device_id_type=pl.DeviceIdType.MESH,
        )

    block = 2 * small

    def chunk(sub, bin_index):
        start = pl.multiple_of((sub * pulses + bin_index) * block, block)
        return outgoing.at[pl.ds(start, block)]

    def landing(sub, slot):
        rows = pl.ds(pl.multiple_of(sub * block, block), block)
        return arrived.at[slot, my_rng, my_chan, rows]

    def turn(phase):
        slot = phase // SUBS
        place = phase - slot * SUBS
        return slot, lax.rem(place + slot // last, SUBS)

    def send(phase):
        slot, sub = turn(phase)

        @pl.loop(0, devices - 1)
        def _(step):
            offset = devices // 2 + step
            offset = offset + (offset >= devices).astype(jnp.int32)
            other = lax.rem(me + offset, devices)
            pltpu.make_async_remote_copy(
                src_ref=chunk(sub, other * own + slot),
                dst_ref=landing(sub, slot),
                send_sem=send_sem.at[slot, sub],
                recv_sem=recv_sem.at[slot, sub],
                device_id={"chan": lax.rem(other, chan_count), "rng": other // chan_count},
                device_id_type=pl.DeviceIdType.MESH,
            ).start()

        pltpu.make_async_copy(
            chunk(sub, me * own + slot), landing(sub, slot), recv_sem.at[slot, sub]
        ).start()

    def wait_sent(phase):
        slot, sub = turn(phase)
        sent = outgoing.at[pl.ds(0, (devices - 1) * block)]
        pltpu.make_async_copy(sent, sent, send_sem.at[slot, sub]).wait()

    def transform(sub):
        @pl.loop(0, small // 8)
        def _(group):
            columns = []
            for lane in range(8):
                channel = sub * small + group * 8 + lane
                columns.append(
                    jnp.concatenate([staged[0, channel], staged[1, channel]], axis=0)
                )
            high, low = halves_of(jnp.concatenate(columns, axis=1))
            spectrum = jnp.dot(
                table_ref[...],
                jnp.concatenate([high, high, low], axis=0),
                preferred_element_type=jnp.float32,
            )
            for side in range(2):
                for lane in range(8):
                    start = sub * pulses * block + side * small + group * 8 + lane
                    outgoing[pl.ds(start, pulses, stride=block), :] = spectrum[
                        side * pulses : (side + 1) * pulses,
                        lane * LANES : (lane + 1) * LANES,
                    ]

    for sub in range(SUBS):
        if sub < 2:
            load(sub).wait()
        transform(sub)
        if sub == 0:
            pl.semaphore_wait(barrier, devices - 1)
        if sub < WINDOW:
            send(jnp.int32(sub))

    phases = own * SUBS

    def advance(phase):
        wait_sent(phase)

        @pl.when(phase + WINDOW < phases)
        def _():
            send(phase + WINDOW)

        slot, sub = turn(phase)
        rows = pl.ds(pl.multiple_of(sub * block, block), block)
        landed = arrived.at[slot, :, :, rows]
        pltpu.make_async_copy(landed, landed, recv_sem.at[slot, sub]).wait()
        convolve(sub, slot)

    spans = gates // SPAN
    reach = band_high.shape[2] // SPAN
    per_span = SPAN // LANES

    def convolve(sub, slot):
        def samples(source, first):
            columns = []
            for rng in range(first * per_span, (first + 1) * per_span):
                rows = pl.ds(pl.multiple_of((2 * sub + source) * small, small), small)
                tile = arrived[slot, rng, :, rows, :]
                columns.append(tile.reshape(chan_count * small, LANES))
            return halves_of(jnp.concatenate(columns, axis=1))

        pairs = [[samples(source, first) for first in range(spans)] for source in range(2)]
        for target in range(spans):
            count = min(reach, spans - target)
            total = jnp.zeros((chan_count * small, 2 * SPAN), jnp.float32)
            for source in range(2):
                taken = pairs[source][target : target + count]
                high = jnp.concatenate([pair[0] for pair in taken], axis=1)
                low = jnp.concatenate([pair[1] for pair in taken], axis=1)
                width = count * SPAN
                total = total + dot_rows(high, band_high[source, :, :width])
                total = total + dot_rows(high, band_low[source, :, :width])
                total = total + dot_rows(low, band_high[source, :, :width])
            high, low = halves_of(total)
            for chan in range(chan_count):
                rows = pl.ds(pl.multiple_of(chan * channels + sub * small, small), small)
                local = slice(chan * small, (chan + 1) * small)
                for side in range(2):
                    start = side * gates + target * SPAN
                    span_cols = slice(side * SPAN, (side + 1) * SPAN)
                    high_ref[rows, start : start + SPAN] = high[local, span_cols]
                    low_ref[rows, start : start + SPAN] = low[local, span_cols]

    def outer(left, right):
        def one(first, second):
            lefts = slice(first * gates, (first + 1) * gates)
            rights = slice(second * gates, (second + 1) * gates)
            total = dot_rows(left[0](lefts), right[0](rights))
            total = total + dot_rows(left[0](lefts), right[1](rights))
            return total + dot_rows(left[1](lefts), right[0](rights))

        scale = 1.0 / gates
        return (one(0, 0) + one(1, 1)) * scale, (one(1, 0) - one(0, 1)) * scale

    def rows_of(first, count):
        rows = pl.ds(pl.multiple_of(first, small), count)
        return tuple(lambda cols, ref=ref: ref[rows, cols] for ref in (high_ref, low_ref))

    every = tuple(lambda cols, ref=ref: ref[:, cols] for ref in (high_ref, low_ref))

    def edge(cols, ref):
        return jnp.concatenate(
            [ref[chan * channels : chan * channels + small, cols] for chan in range(chan_count)],
            axis=0,
        )

    edges = tuple(lambda cols, ref=ref: edge(cols, ref) for ref in (high_ref, low_ref))

    def owner_at(step):
        half = chan_count // 2
        offset = jnp.where(step < half, half + step, chan_count - 1 - step)
        return lax.rem(my_chan + offset, chan_count)

    def hand_over(owner, source, target, send_to, recv_from):
        @pl.when(owner != my_chan)
        def _():
            pltpu.make_async_remote_copy(
                src_ref=source,
                dst_ref=target,
                send_sem=send_to,
                recv_sem=recv_from,
                device_id={"chan": owner, "rng": my_rng},
                device_id_type=pl.DeviceIdType.MESH,
            ).start()

        @pl.when(owner == my_chan)
        def _():
            pltpu.make_async_copy(source, target, recv_from).start()

    for slot in range(last):
        @pl.loop(slot * SUBS, (slot + 1) * SUBS)
        def _(phase):
            advance(phase)

        @pl.loop(0, chan_count)
        def _(step):
            owner = owner_at(step)
            real, imag = outer(rows_of(owner * channels, channels), every)
            rows_ref[slot, owner, 0] = real
            rows_ref[slot, owner, 1] = imag
            hand_over(
                owner,
                rows_ref.at[slot, owner],
                out_ref.at[:, my_chan * own + slot],
                row_send_sem.at[slot],
                row_recv_sem.at[slot],
            )

    @pl.loop(last * SUBS, phases - 1)
    def _(phase):
        advance(phase)

    @pl.loop(0, chan_count)
    def _(step):
        owner = owner_at(step)
        real, imag = outer(rows_of(owner * channels + small, big), every)
        rows_ref[last, owner, 0, small:, :] = real
        rows_ref[last, owner, 1, small:, :] = imag
        hand_over(
            owner,
            rows_ref.at[last, owner, :, pl.ds(small, big)],
            early_ref.at[my_chan],
            early_sem.at[0],
            early_sem.at[1],
        )

    advance(jnp.int32(phases - 1))
    real, imag = outer(edges, every)
    for chan in range(chan_count):
        local = slice(chan * small, (chan + 1) * small)
        rows_ref[last, chan, 0, :small, :] = real[local]
        rows_ref[last, chan, 1, :small, :] = imag[local]

    @pl.loop(0, chan_count)
    def _(step):
        owner = owner_at(step)
        hand_over(
            owner,
            rows_ref.at[last, owner, :, pl.ds(0, small)],
            out_ref.at[:, my_chan * own + last, pl.ds(0, small)],
            row_send_sem.at[last],
            row_recv_sem.at[last],
        )

    @pl.loop(0, chan_count)
    def _(step):
        owner = owner_at(step)
        real, imag = outer(rows_of(owner * channels + small, big), edges)
        edge_ref[owner, 0] = real
        edge_ref[owner, 1] = imag
        hand_over(
            owner, edge_ref.at[owner], late_ref.at[my_chan], late_sem.at[0], late_sem.at[1]
        )

    pltpu.make_async_copy(early_ref, early_ref, early_sem.at[1]).wait()
    pltpu.make_async_copy(late_ref, late_ref, late_sem.at[1]).wait()
    width = chan_count * small
    lanes = lax.broadcasted_iota(jnp.int32, (big, width), 1)
    for chan in range(chan_count):
        for side in range(2):
            late = late_ref[chan, side]
            for tile in range(chan_count):
                cols = slice(tile * channels, (tile + 1) * channels)
                moved = pltpu.roll(late, (width - tile * small) % width, 1)
                early_ref[chan, side, :, cols] = jnp.where(
                    lanes < small, moved, early_ref[chan, side, :, cols]
                )

    def deliver(chan):
        return pltpu.make_async_copy(
            early_ref.at[chan],
            out_ref.at[:, chan * own + last, pl.ds(small, big)],
            load_sem.at[chan],
        )

    for chan in range(chan_count):
        deliver(chan).start()
    others = pl.ds(0, chan_count - 1)
    bins = pl.ds(0, chan_count)
    for slot in range(last):
        given = rows_ref.at[slot, others]
        pltpu.make_async_copy(given, given, row_send_sem.at[slot]).wait()
        taken = out_ref.at[:, bins]
        pltpu.make_async_copy(taken, taken, row_recv_sem.at[slot]).wait()
    given = rows_ref.at[last, others, :, pl.ds(0, small)]
    pltpu.make_async_copy(given, given, row_send_sem.at[last]).wait()
    taken = out_ref.at[:, bins, pl.ds(0, small)]
    pltpu.make_async_copy(taken, taken, row_recv_sem.at[last]).wait()
    given = early_ref.at[others]
    pltpu.make_async_copy(given, given, early_sem.at[0]).wait()
    given = edge_ref.at[others]
    pltpu.make_async_copy(given, given, late_sem.at[0]).wait()
    for chan in range(chan_count):
        deliver(chan).wait()


def by_bins(echoes, filter_taps, rng_count, chan_count):
    channels, pulses, part = echoes.shape[1:]
    gates = part * rng_count
    own = pulses // (rng_count * chan_count)
    small = channels // SUBS
    big = channels - small
    whole = channels * chan_count
    sizes = (rng_count, chan_count, own, channels, pulses, gates)
    band_high, band_low = band_tables(filter_taps)
    vmem = pl.BlockSpec(memory_space=pltpu.VMEM)
    hbm = pl.BlockSpec(memory_space=pl.ANY)
    return pl.pallas_call(
        functools.partial(dwell_kernel, sizes),
        out_shape=jax.ShapeDtypeStruct((2, own * chan_count, channels, whole), jnp.float32),
        in_specs=[hbm, vmem, vmem, vmem],
        out_specs=hbm,
        scratch_shapes=[
            pltpu.VMEM(echoes.shape, jnp.float32),
            pltpu.VMEM((2 * pulses * channels, part), jnp.float32),
            pltpu.VMEM((own, rng_count, chan_count, 2 * channels, part), jnp.float32),
            pltpu.VMEM((whole, 2 * gates), jnp.bfloat16),
            pltpu.VMEM((whole, 2 * gates), jnp.bfloat16),
            pltpu.VMEM((own, chan_count, 2, channels, whole), jnp.float32),
            pltpu.VMEM((chan_count, 2, big, whole), jnp.float32),
            pltpu.VMEM((chan_count, 2, big, chan_count * small), jnp.float32),
            pltpu.VMEM((chan_count, 2, big, chan_count * small), jnp.float32),
            pltpu.SemaphoreType.DMA((max(2, chan_count),)),
            pltpu.SemaphoreType.DMA((own, SUBS)),
            pltpu.SemaphoreType.DMA((own, SUBS)),
            pltpu.SemaphoreType.DMA((own,)),
            pltpu.SemaphoreType.DMA((own,)),
            pltpu.SemaphoreType.DMA((2,)),
            pltpu.SemaphoreType.DMA((2,)),
        ],
        compiler_params=pltpu.CompilerParams(
            collective_id=0, has_side_effects=True, vmem_limit_bytes=56 * MIB
        ),
    )(echoes, jnp.asarray(doppler_table(pulses)), band_high, band_low)


def solution(mesh):
    rng_count = mesh.shape["rng"]
    chan_count = mesh.shape["chan"]

    def per_device(echoes, filter_taps):
        channels, pulses, part = echoes.shape[1:]
        fits = (
            pulses % (rng_count * chan_count) == 0
            and pulses >= 2 * rng_count * chan_count
            and chan_count == SUBS
            and channels == LANES
            and part == LANES
            and (part * rng_count) % SPAN == 0
            and filter_taps.shape[1] % SPAN == 0
        )
        if fits:
            return by_bins(echoes, filter_taps, rng_count, chan_count)
        return by_gates(echoes, filter_taps)

    in_specs = (P(None, "chan", None, "rng"), P())
    out_specs = P(None, "rng", "chan", None)
    return jax.shard_map(
        per_device, mesh=mesh, in_specs=in_specs, out_specs=out_specs, check_vma=False
    )
```
